256 devices in a mesh: dp: 64 (over y_lo, z, x), mp: 4 (over y_hi, core).
Axes of the slice: x: 4, y: 4 (y_hi: 2, y_lo: 2; y = y_hi * 2 + y_lo), z: 8, core: 2. Of those that a mesh axis runs over, the one named last changes fastest.
Arguments:
- activations: bfloat16 [4, 128, 256, 2048], P(None, 'dp', None, 'mp'), may hold values from -6 to 6
- out_grads: bfloat16 [4, 128, 256, 8192], P(None, 'dp', None, 'mp'), may hold values from -6 to 6
- proj_in: bfloat16 [4, 64, 2048], P(None, None, 'mp'), may hold values from -0.125 to 0.125
- proj_out: bfloat16 [4, 64, 8192], P(None, None, 'mp'), may hold values from -0.0625 to 0.0625
- query_grads: float32 [4, 64, 64, 64], P(None, 'dp'), may hold values from -6 to 6
Outputs:
- scores: float32 [128, 64], P('dp')
The draws below stay inside these ranges and needn't reach their ends.
All inputs are finite; a program needn't handle non-finite values.
Results may differ from the reference program's by a relative error of at most 0.0003.
Values sent between devices are 32-bit elements; how exact they have to be, the bound alone decides.
No kernel may reach another device: no remote copies, remote signals or barrier semaphores. Data moves between devices by JAX's collectives and lax.ppermute only.
A program may use at most 128 MiB of HBM per device.

```python
import jax
import jax.numpy as jnp
from jax import lax

D = 2048
FF = 8192
K = 64
LAYERS = 4
FRAMES = 256
QUERIES = 64
CLIPS = 128


def block_levels(own_key, dims, cuts, smallest, largest):
    loudness, own = 1.0, jax.random.fold_in(own_key, 6)
    for axis_at, parts in cuts:
        draws = jnp.exp(jax.random.uniform(jax.random.fold_in(own, axis_at), (parts,), jnp.float32, smallest / len(cuts), largest / len(cuts)))
        loudness = loudness * jnp.repeat(draws, dims[axis_at] // parts).reshape([-1 if axis == axis_at else 1 for axis in range(len(dims))])
    return loudness


def bell_draw(own_key, shape, scale, bound, shards=(), kind=jnp.bfloat16):
    loudness = block_levels(own_key, shape, shards, -0.22, 0.18) if shards else 1.0
    entries = jax.random.normal(own_key, shape, jnp.float32) * scale * loudness
    return jnp.minimum(jnp.maximum(entries, -bound), bound).astype(kind)


def setup_inputs(seed: int = 0) -> dict:
    key_of = jax.random.split(jax.random.key(seed), 6)
    activations = bell_draw(key_of[0], (LAYERS, CLIPS, FRAMES, D), 1.0, 6.0, ((1, 64), (3, 4)))
    out_grads = bell_draw(key_of[1], (LAYERS, CLIPS, FRAMES, FF), 1.0, 6.0, ((1, 64), (3, 4)))
    proj_in = bell_draw(key_of[2], (LAYERS, K, D), D ** -0.5, 0.125, ((2, 4),))
    proj_out = bell_draw(key_of[3], (LAYERS, K, FF), FF ** -0.5, 0.0625, ((2, 4),))
    query_grads = bell_draw(key_of[4], (LAYERS, QUERIES, K, K), 1.0, 6.0, ((1, 64),), jnp.float32)
    return {"activations": activations, "out_grads": out_grads, "proj_in": proj_in, "proj_out": proj_out, "query_grads": query_grads}


DAMP = 0.1

def precondition(fac_in, fac_out, queries):
    width = fac_in.shape[0]
    eye = jnp.eye(width, dtype=jnp.float32)
    damped_in = fac_in + DAMP * jnp.trace(fac_in) / width * eye
    damped_out = fac_out + DAMP * jnp.trace(fac_out) / width * eye
    chol_in = jnp.linalg.cholesky(damped_in)
    chol_out = jnp.linalg.cholesky(damped_out)
    left = jax.vmap(lambda block: jax.scipy.linalg.cho_solve((chol_in, True), block))(queries)
    return jax.vmap(lambda block: jax.scipy.linalg.cho_solve((chol_out, True), block.T).T)(left)

def reference(activations, out_grads, proj_in, proj_out, query_grads):
    total = CLIPS * FRAMES
    scores = jnp.zeros((CLIPS, QUERIES), jnp.float32)
    for layer in range(LAYERS):
        flat_x = activations[layer].reshape(total, D)
        flat_g = out_grads[layer].reshape(total, FF)
        xp = jnp.dot(flat_x.astype(jnp.float32), proj_in[layer].T.astype(jnp.float32), preferred_element_type=jnp.float32)
        gp = jnp.dot(flat_g.astype(jnp.float32), proj_out[layer].T.astype(jnp.float32), preferred_element_type=jnp.float32)
        fac_in = jnp.dot(xp.T, xp, precision=lax.Precision.HIGHEST) / total
        fac_out = jnp.dot(gp.T, gp, precision=lax.Precision.HIGHEST) / total
        clip_grads = jnp.einsum('cfi,cfj->cij', xp.reshape(CLIPS, FRAMES, K), gp.reshape(CLIPS, FRAMES, K), precision=lax.Precision.HIGHEST) / jnp.sqrt(jnp.float32(FRAMES))
        conditioned = precondition(fac_in, fac_out, query_grads[layer])
        scores = scores + jnp.einsum('cij,qij->cq', clip_grads, conditioned, precision=lax.Precision.HIGHEST)
    return scores / jnp.sqrt(jnp.float32(LAYERS * K * K))
```

```python
import functools

import jax
import jax.numpy as jnp
from jax import lax
from jax.experimental import pallas as pl
from jax.experimental.pallas import tpu as pltpu
from jax.sharding import PartitionSpec as P

DAMP = 0.1
QUERY_VMEM = 56426496
VMEM = 53 * 2**20 + 2**19
QUERY_BITS = (8, 24, 4, 32, 1, 3)
QUERY_AT = {1: 3, 2: 4, 4: 5}
FACTOR_BITS = (1, 3, 4, 8, 24, 32)
HIGH = lax.Precision.HIGHEST


def xor_pairs(size, bit):
    return [(i, i ^ bit) for i in range(size)]


def project_kernel(offset, has_query, x_hbm, g_hbm, pi_hbm, po_hbm, *rest):
    if has_query:
        query_hbm, out, own, xs, gs, pis, pos, sems, block, query_sem = rest
    else:
        out, xs, gs, pis, pos, sems = rest
    rows, wide = out.shape
    rank = wide // 2
    me = lax.axis_index("mp")
    layer = me ^ offset
    copies = [
        pltpu.make_async_copy(source.at[layer], target, sems.at[index])
        for index, (source, target) in enumerate(
            ((pi_hbm, pis), (x_hbm, xs), (po_hbm, pos), (g_hbm, gs))
        )
    ]
    if has_query:
        fetch = pltpu.make_async_copy(query_hbm.at[me, 0], block, query_sem)
        fetch.start()
    for copy in copies:
        copy.start()
    for copy in copies:
        copy.wait()
    contract = (((1,), (1,)), ((), ()))
    out[:, :rank] = lax.dot_general(
        xs[...].reshape(rows, xs.shape[2]), pis[...], contract, preferred_element_type=jnp.float32
    )
    out[:, rank:] = lax.dot_general(
        gs[...].reshape(rows, gs.shape[2]), pos[...], contract, preferred_element_type=jnp.float32
    )
    if has_query:
        fetch.wait()
        own[0, :, :rank] = block[: rank // 2]
        own[0, :, rank:] = block[rank // 2 :]


def project(offset, args, query=None, after=None):
    activations, out_grads, proj_in, proj_out = args
    if after is not None:
        proj_in, _ = lax.optimization_barrier((proj_in, after))
    _, clips, frames, width = activations.shape
    hidden = out_grads.shape[3]
    rank = proj_in.shape[1]
    rows = clips * frames
    kind = activations.dtype
    anywhere = pl.BlockSpec(memory_space=pl.ANY)
    vmem = pl.BlockSpec(memory_space=pltpu.VMEM)
    out_shape = jax.ShapeDtypeStruct((rows, 2 * rank), jnp.float32)
    scratch = [
        pltpu.VMEM((clips, frames, width), kind),
        pltpu.VMEM((clips, frames, hidden), kind),
        pltpu.VMEM((rank, width), kind),
        pltpu.VMEM((rank, hidden), kind),
        pltpu.SemaphoreType.DMA((4,)),
    ]
    operands, out_specs = [activations, out_grads, proj_in, proj_out], vmem
    if query is not None:
        operands.append(query)
        out_specs = [vmem, vmem]
        out_shape = [out_shape, jax.ShapeDtypeStruct((1, rank // 2, 2 * rank), jnp.float32)]
        scratch += [pltpu.VMEM((rank, rank), jnp.float32), pltpu.SemaphoreType.DMA]
    return pl.pallas_call(
        functools.partial(project_kernel, offset, query is not None),
        in_specs=[anywhere] * len(operands),
        out_specs=out_specs,
        out_shape=out_shape,
        scratch_shapes=scratch,
        compiler_params=pltpu.CompilerParams(vmem_limit_bytes=VMEM if query is None else QUERY_VMEM),
        cost_estimate=pl.CostEstimate(
            flops=rows * (width + hidden) * rank * 2,
            bytes_accessed=rows * (width + hidden) * 2 + rows * rank * 8,
            transcendentals=0,
        ),
        name="project",
    )(*operands)


def moments_kernel(clips, a_ref, b_ref, fac_ref, grad_ref):
    z = a_ref[...] + b_ref[...]
    rows, wide = z.shape
    rank = wide // 2
    frames = rows // clips
    total = None
    for clip in range(clips):
        part = z[clip * frames : (clip + 1) * frames]
        moment = lax.dot_general(
            part, part, (((0,), (0,)), ((), ())), precision=HIGH, preferred_element_type=jnp.float32
        )
        total = moment if total is None else total + moment
        grad_ref[:, clip * rank : (clip + 1) * rank] = moment[:rank, rank:]
    fac_ref[:, :rank] = total[:rank, :rank]
    fac_ref[:, rank:] = total[rank:, rank:]


def moments(clips, a, b):
    rows, wide = a.shape
    rank = wide // 2
    return pl.pallas_call(
        functools.partial(moments_kernel, clips),
        out_shape=[
            jax.ShapeDtypeStruct((rank, wide), jnp.float32),
            jax.ShapeDtypeStruct((rank, clips * rank), jnp.float32),
        ],
        compiler_params=pltpu.CompilerParams(vmem_limit_bytes=8 * 2**20),
        name="moments",
    )(a, b)


def solve_kernel(clips, total, fa_ref, fb_ref, grad_ref, out_ref):
    rank, wide = fa_ref.shape
    half = rank // 2
    fac = (fa_ref[...] + fb_ref[...]) * (1.0 / total)
    row = lax.broadcasted_iota(jnp.int32, (rank, wide), 0)
    lane = lax.broadcasted_iota(jnp.int32, (rank, wide), 1)
    left = lane < rank
    eye = (row == lane) | (row + rank == lane)
    diag = jnp.where(eye, fac, 0.0)
    trace_l = jnp.sum(jnp.where(left, diag, 0.0))
    trace_r = jnp.sum(jnp.where(left, 0.0, diag))
    damp = jnp.where(left, trace_l, trace_r) * (DAMP / rank)
    mat = fac + jnp.where(eye, damp, 0.0)
    def column(source, k):
        return jnp.where(left, source[:, k : k + 1], source[:, rank + k : rank + k + 1])

    c0, c1 = column(mat, 0), column(mat, 1)
    for k in range(0, rank, 2):
        ahead = [column(mat, j) for j in (k + 2, k + 3) if j < rank]
        a, b, d = c0[k : k + 1], c0[k + 1 : k + 2], c1[k + 1 : k + 2]
        at0 = (lane == k) | (lane == rank + k)
        at1 = (lane == k + 1) | (lane == rank + k + 1)
        scale = 1.0 / (a * d - b * b)
        a, b, d = a * scale, b * scale, d * scale
        r0 = jnp.where(at0[:1], 1.0, jnp.where(at1[:1], 0.0, mat[k : k + 1]))
        r1 = jnp.where(at1[:1], 1.0, jnp.where(at0[:1], 0.0, mat[k + 1 : k + 2]))
        n0 = d * r0 - b * r1
        n1 = a * r1 - b * r0
        rest = jnp.where(at0 | at1, 0.0, mat) - c0 * n0 - c1 * n1
        mat = jnp.where(row == k, n0, jnp.where(row == k + 1, n1, rest))
        following = []
        for col in ahead:
            u, v = col[k : k + 1], col[k + 1 : k + 2]
            m0 = d * u - b * v
            m1 = a * v - b * u
            rest = col - c0 * m0 - c1 * m1
            following.append(jnp.where(row == k, m0, jnp.where(row == k + 1, m1, rest)))
        if following:
            c0, c1 = following
    inv_in = mat[:, :rank]
    inv_out = mat[:, rank:]
    left_solved = jnp.dot(inv_in, grad_ref[...], precision=HIGH, preferred_element_type=jnp.float32)
    for clip in range(clips):
        solved = jnp.dot(
            left_solved[:, clip * rank : (clip + 1) * rank], inv_out, precision=HIGH,
            preferred_element_type=jnp.float32,
        )
        out_ref[clip, :, :rank] = solved[:half]
        out_ref[clip, :, rank:] = solved[half:]


def solve(clips, total, fa, fb, grads):
    rank, wide = fa.shape
    vmem = pl.BlockSpec(memory_space=pltpu.VMEM)
    return pl.pallas_call(
        functools.partial(solve_kernel, clips, total),
        in_specs=[vmem] * 3,
        out_specs=vmem,
        out_shape=jax.ShapeDtypeStruct((clips, rank // 2, wide), jnp.float32),
        compiler_params=pltpu.CompilerParams(vmem_limit_bytes=8 * 2**20),
        cost_estimate=pl.CostEstimate(flops=0, bytes_accessed=8_000_000, transcendentals=0),
        name="solve",
    )(fa, fb, grads)


def contract_kernel(scale, solved_ref, q_ref, out_ref):
    at = lax.axis_index("dp").astype(jnp.int32)
    queries, half, wide = q_ref.shape
    clips = solved_ref.shape[0]
    q_at = lax.broadcasted_iota(jnp.int32, (queries, queries * 8), 0)
    r_at = lax.broadcasted_iota(jnp.int32, (queries, queries * 8), 1) // 8
    came = at
    for index, bit in enumerate(QUERY_BITS):
        came = came ^ jnp.where((r_at >> index) & 1 == 1, bit, 0)
    select = jnp.where(came == q_at, 1.0, 0.0)
    q = q_ref[...].reshape(queries, half // 8, 8, wide)
    partial = jnp.concatenate(
        [
            jnp.sum(q * solved_ref[clip].reshape(1, half // 8, 8, wide), axis=1).reshape(
                queries * 8, wide
            )
            for clip in range(clips)
        ],
        axis=1,
    )
    per_query = jnp.dot(select, partial, precision=HIGH, preferred_element_type=jnp.float32)
    ones = jnp.full((8, wide), scale, jnp.float32)
    for clip in range(clips):
        line = lax.dot_general(
            ones, per_query[:, clip * wide : (clip + 1) * wide], (((1,), (1,)), ((), ())),
            precision=HIGH, preferred_element_type=jnp.float32,
        )
        out_ref[clip : clip + 1, :] = line[:1]


def contract(scale, solved, queries):
    vmem = pl.BlockSpec(memory_space=pltpu.VMEM)
    return pl.pallas_call(
        functools.partial(contract_kernel, scale),
        in_specs=[vmem] * 2,
        out_specs=vmem,
        out_shape=jax.ShapeDtypeStruct((solved.shape[0], queries.shape[0]), jnp.float32),
        compiler_params=pltpu.CompilerParams(vmem_limit_bytes=16 * 2**20),
        name="contract",
    )(solved, queries)


def local(activations, out_grads, proj_in, proj_out, query_grads):
    layers, clips, frames, _ = activations.shape
    rank = proj_in.shape[1]
    members = lax.axis_size("mp")
    groups = lax.axis_size("dp")
    me = lax.axis_index("mp")

    def widen(blocks, index, after):
        blocks, _ = lax.optimization_barrier((blocks, after))
        pairs = xor_pairs(groups, QUERY_BITS[index])
        return jnp.concatenate([blocks, lax.ppermute(blocks, "dp", pairs)])

    args = (activations, out_grads, proj_in, proj_out)
    far, gathered = project(3, args, query=query_grads)
    far_in = lax.ppermute(far, "mp", xor_pairs(members, 1))
    cross = project(2, args, after=far) + far_in
    cross_in = lax.ppermute(cross, "mp", xor_pairs(members, 2))
    near = project(1, args, after=cross)
    near_in = lax.ppermute(near, "mp", xor_pairs(members, 1))
    mine = project(0, args, after=near)
    gathered = widen(gathered, 0, far)
    gathered = widen(gathered, 1, near)
    gathered = widen(gathered, 2, mine)
    fac, grads = moments(clips, mine + cross_in, near_in)
    for step, bit in enumerate(FACTOR_BITS[:-1]):
        if step in QUERY_AT:
            gathered = widen(gathered, QUERY_AT[step], fac)
        fac = fac + lax.ppermute(fac, "dp", xor_pairs(groups, bit))
    other = lax.ppermute(fac, "dp", xor_pairs(groups, FACTOR_BITS[-1]))
    solved = solve(clips, clips * frames * groups, fac, other, grads)
    scale = 1.0 / (frames**0.5 * (layers * rank * rank) ** 0.5)
    out = contract(scale, solved, gathered)
    out = out + lax.ppermute(out, "mp", xor_pairs(members, 1))
    return out + lax.ppermute(out, "mp", xor_pairs(members, 2))


def solution(mesh):
    placed = (
        P(None, "dp", None, "mp"),
        P(None, "dp", None, "mp"),
        P(None, None, "mp"),
        P(None, None, "mp"),
        P(None, "dp", None, None),
    )
    return jax.shard_map(
        local, mesh=mesh, in_specs=placed, out_specs=P("dp", None), check_vma=False
    )
```

```python
import functools

import jax
import jax.numpy as jnp
from jax import lax
from jax.experimental import pallas as pl
from jax.experimental.pallas import tpu as pltpu
from jax.sharding import PartitionSpec as P

DAMP = 0.1
QUERY_VMEM = 56426496
VMEM = 53 * 2**20 + 2**19
QUERY_BITS = (8, 4, 24, 32, 1, 3)
QUERY_AT = {1: 3, 2: 4, 4: 5}
FACTOR_BITS = (1, 3, 4, 24, 8, 32)
HIGH = lax.Precision.HIGHEST


def xor_pairs(size, bit):
    return [(i, i ^ bit) for i in range(size)]


def project_kernel(offset, has_query, x_hbm, g_hbm, pi_hbm, po_hbm, *rest):
    if has_query:
        query_hbm, out, own, xs, gs, pis, pos, sems, block, query_sem = rest
    else:
        out, xs, gs, pis, pos, sems = rest
    rows, wide = out.shape
    rank = wide // 2
    me = lax.axis_index("mp")
    layer = me ^ offset
    copies = [
        pltpu.make_async_copy(source.at[layer], target, sems.at[index])
        for index, (source, target) in enumerate(
            ((pi_hbm, pis), (x_hbm, xs), (po_hbm, pos), (g_hbm, gs))
        )
    ]
    if has_query:
        fetch = pltpu.make_async_copy(query_hbm.at[me, 0], block, query_sem)
        fetch.start()
    for copy in copies:
        copy.start()
    contract = (((1,), (1,)), ((), ()))
    copies[0].wait()
    copies[1].wait()
    out[:, :rank] = lax.dot_general(
        xs[...].reshape(rows, xs.shape[2]), pis[...], contract, preferred_element_type=jnp.float32
    )
    copies[2].wait()
    copies[3].wait()
    out[:, rank:] = lax.dot_general(
        gs[...].reshape(rows, gs.shape[2]), pos[...], contract, preferred_element_type=jnp.float32
    )
    if has_query:
        fetch.wait()
        own[0, :, :rank] = block[: rank // 2]
        own[0, :, rank:] = block[rank // 2 :]


def project(offset, args, query=None, after=None):
    activations, out_grads, proj_in, proj_out = args
    if after is not None:
        proj_in, _ = lax.optimization_barrier((proj_in, after))
    _, clips, frames, width = activations.shape
    hidden = out_grads.shape[3]
    rank = proj_in.shape[1]
    rows = clips * frames
    kind = activations.dtype
    anywhere = pl.BlockSpec(memory_space=pl.ANY)
    vmem = pl.BlockSpec(memory_space=pltpu.VMEM)
    out_shape = jax.ShapeDtypeStruct((rows, 2 * rank), jnp.float32)
    scratch = [
        pltpu.VMEM((clips, frames, width), kind),
        pltpu.VMEM((clips, frames, hidden), kind),
        pltpu.VMEM((rank, width), kind),
        pltpu.VMEM((rank, hidden), kind),
        pltpu.SemaphoreType.DMA((4,)),
    ]
    operands, out_specs = [activations, out_grads, proj_in, proj_out], vmem
    if query is not None:
        operands.append(query)
        out_specs = [vmem, vmem]
        out_shape = [out_shape, jax.ShapeDtypeStruct((1, rank // 2, 2 * rank), jnp.float32)]
        scratch += [pltpu.VMEM((rank, rank), jnp.float32), pltpu.SemaphoreType.DMA]
    return pl.pallas_call(
        functools.partial(project_kernel, offset, query is not None),
        in_specs=[anywhere] * len(operands),
        out_specs=out_specs,
        out_shape=out_shape,
        scratch_shapes=scratch,
        compiler_params=pltpu.CompilerParams(vmem_limit_bytes=VMEM if query is None else QUERY_VMEM),
        cost_estimate=pl.CostEstimate(
            flops=rows * (width + hidden) * rank * 2,
            bytes_accessed=rows * (width + hidden) * 2 + rows * rank * 8,
            transcendentals=0,
        ),
        name="project",
    )(*operands)


def moments_kernel(clips, a_ref, b_ref, fac_ref, grad_ref):
    z = a_ref[...] + b_ref[...]
    rows, wide = z.shape
    rank = wide // 2
    frames = rows // clips
    total = None
    for clip in range(clips):
        part = z[clip * frames : (clip + 1) * frames]
        moment = lax.dot_general(
            part, part, (((0,), (0,)), ((), ())), precision=HIGH, preferred_element_type=jnp.float32
        )
        total = moment if total is None else total + moment
        grad_ref[:, clip * rank : (clip + 1) * rank] = moment[:rank, rank:]
    fac_ref[:, :rank] = total[:rank, :rank]
    fac_ref[:, rank:] = total[rank:, rank:]


def moments(clips, a, b):
    rows, wide = a.shape
    rank = wide // 2
    return pl.pallas_call(
        functools.partial(moments_kernel, clips),
        out_shape=[
            jax.ShapeDtypeStruct((rank, wide), jnp.float32),
            jax.ShapeDtypeStruct((rank, clips * rank), jnp.float32),
        ],
        compiler_params=pltpu.CompilerParams(vmem_limit_bytes=8 * 2**20),
        name="moments",
    )(a, b)


def solve_kernel(clips, total, fa_ref, fb_ref, grad_ref, out_ref):
    rank, wide = fa_ref.shape
    half = rank // 2
    fac = (fa_ref[...] + fb_ref[...]) * (1.0 / total)
    row = lax.broadcasted_iota(jnp.int32, (rank, wide), 0)
    lane = lax.broadcasted_iota(jnp.int32, (rank, wide), 1)
    left = lane < rank
    eye = (row == lane) | (row + rank == lane)
    diag = jnp.where(eye, fac, 0.0)
    trace_l = jnp.sum(jnp.where(left, diag, 0.0))
    trace_r = jnp.sum(jnp.where(left, 0.0, diag))
    damp = jnp.where(left, trace_l, trace_r) * (DAMP / rank)
    mat = fac + jnp.where(eye, damp, 0.0)
    def column(source, k):
        return jnp.where(left, source[:, k : k + 1], source[:, rank + k : rank + k + 1])

    c0, c1 = column(mat, 0), column(mat, 1)
    for k in range(0, rank, 2):
        ahead = [column(mat, j) for j in (k + 2, k + 3) if j < rank]
        a, b, d = c0[k : k + 1], c0[k + 1 : k + 2], c1[k + 1 : k + 2]
        at0 = (lane == k) | (lane == rank + k)
        at1 = (lane == k + 1) | (lane == rank + k + 1)
        scale = 1.0 / (a * d - b * b)
        a, b, d = a * scale, b * scale, d * scale
        r0 = jnp.where(at0[:1], 1.0, jnp.where(at1[:1], 0.0, mat[k : k + 1]))
        r1 = jnp.where(at1[:1], 1.0, jnp.where(at0[:1], 0.0, mat[k + 1 : k + 2]))
        n0 = d * r0 - b * r1
        n1 = a * r1 - b * r0
        rest = jnp.where(at0 | at1, 0.0, mat) - c0 * n0 - c1 * n1
        mat = jnp.where(row == k, n0, jnp.where(row == k + 1, n1, rest))
        following = []
        for col in ahead:
            u, v = col[k : k + 1], col[k + 1 : k + 2]
            m0 = d * u - b * v
            m1 = a * v - b * u
            rest = col - c0 * m0 - c1 * m1
            following.append(jnp.where(row == k, m0, jnp.where(row == k + 1, m1, rest)))
        if following:
            c0, c1 = following
    inv_in = mat[:, :rank]
    inv_out = mat[:, rank:]
    left_solved = jnp.dot(inv_in, grad_ref[...], precision=HIGH, preferred_element_type=jnp.float32)
    for clip in range(clips):
        solved = jnp.dot(
            left_solved[:, clip * rank : (clip + 1) * rank], inv_out, precision=HIGH,
            preferred_element_type=jnp.float32,
        )
        out_ref[clip, :, :rank] = solved[:half]
        out_ref[clip, :, rank:] = solved[half:]


def solve(clips, total, fa, fb, grads):
    rank, wide = fa.shape
    vmem = pl.BlockSpec(memory_space=pltpu.VMEM)
    return pl.pallas_call(
        functools.partial(solve_kernel, clips, total),
        in_specs=[vmem] * 3,
        out_specs=vmem,
        out_shape=jax.ShapeDtypeStruct((clips, rank // 2, wide), jnp.float32),
        compiler_params=pltpu.CompilerParams(vmem_limit_bytes=8 * 2**20),
        cost_estimate=pl.CostEstimate(flops=0, bytes_accessed=8_000_000, transcendentals=0),
        name="solve",
    )(fa, fb, grads)


def contract_kernel(scale, solved_ref, q_ref, out_ref):
    at = lax.axis_index("dp").astype(jnp.int32)
    queries, half, wide = q_ref.shape
    clips = solved_ref.shape[0]
    q_at = lax.broadcasted_iota(jnp.int32, (queries, queries * 8), 0)
    r_at = lax.broadcasted_iota(jnp.int32, (queries, queries * 8), 1) // 8
    came = at
    for index, bit in enumerate(QUERY_BITS):
        came = came ^ jnp.where((r_at >> index) & 1 == 1, bit, 0)
    select = jnp.where(came == q_at, 1.0, 0.0)
    q = q_ref[...].reshape(queries, half // 8, 8, wide)
    partial = jnp.concatenate(
        [
            jnp.sum(q * solved_ref[clip].reshape(1, half // 8, 8, wide), axis=1).reshape(
                queries * 8, wide
            )
            for clip in range(clips)
        ],
        axis=1,
    )
    per_query = jnp.dot(select, partial, precision=HIGH, preferred_element_type=jnp.float32)
    ones = jnp.full((8, wide), scale, jnp.float32)
    for clip in range(clips):
        line = lax.dot_general(
            ones, per_query[:, clip * wide : (clip + 1) * wide], (((1,), (1,)), ((), ())),
            precision=HIGH, preferred_element_type=jnp.float32,
        )
        out_ref[clip : clip + 1, :] = line[:1]


def contract(scale, solved, queries):
    vmem = pl.BlockSpec(memory_space=pltpu.VMEM)
    return pl.pallas_call(
        functools.partial(contract_kernel, scale),
        in_specs=[vmem] * 2,
        out_specs=vmem,
        out_shape=jax.ShapeDtypeStruct((solved.shape[0], queries.shape[0]), jnp.float32),
        compiler_params=pltpu.CompilerParams(vmem_limit_bytes=16 * 2**20),
        name="contract",
    )(solved, queries)


def local(activations, out_grads, proj_in, proj_out, query_grads):
    layers, clips, frames, _ = activations.shape
    rank = proj_in.shape[1]
    members = lax.axis_size("mp")
    groups = lax.axis_size("dp")
    me = lax.axis_index("mp")

    def widen(blocks, index, after):
        blocks, _ = lax.optimization_barrier((blocks, after))
        pairs = xor_pairs(groups, QUERY_BITS[index])
        return jnp.concatenate([blocks, lax.ppermute(blocks, "dp", pairs)])

    args = (activations, out_grads, proj_in, proj_out)
    far, gathered = project(3, args, query=query_grads)
    far_in = lax.ppermute(far, "mp", xor_pairs(members, 1))
    cross = project(2, args, after=far) + far_in
    cross_in = lax.ppermute(cross, "mp", xor_pairs(members, 2))
    near = project(1, args, after=cross)
    near_in = lax.ppermute(near, "mp", xor_pairs(members, 1))
    mine = project(0, args, after=near)
    gathered = widen(gathered, 0, far)
    gathered = widen(gathered, 1, near)
    gathered = widen(gathered, 2, mine)
    fac, grads = moments(clips, mine + cross_in, near_in)
    for step, bit in enumerate(FACTOR_BITS[:-1]):
        if step in QUERY_AT:
            gathered = widen(gathered, QUERY_AT[step], fac)
        fac = fac + lax.ppermute(fac, "dp", xor_pairs(groups, bit))
    other = lax.ppermute(fac, "dp", xor_pairs(groups, FACTOR_BITS[-1]))
    solved = solve(clips, clips * frames * groups, fac, other, grads)
    scale = 1.0 / (frames**0.5 * (layers * rank * rank) ** 0.5)
    out = contract(scale, solved, gathered)
    out = out + lax.ppermute(out, "mp", xor_pairs(members, 1))
    return out + lax.ppermute(out, "mp", xor_pairs(members, 2))


def solution(mesh):
    placed = (
        P(None, "dp", None, "mp"),
        P(None, "dp", None, "mp"),
        P(None, None, "mp"),
        P(None, None, "mp"),
        P(None, "dp", None, None),
    )
    return jax.shard_map(
        local, mesh=mesh, in_specs=placed, out_specs=P("dp", None), check_vma=False
    )
```

```python
import functools

import jax
import jax.numpy as jnp
from jax import lax
from jax.experimental import pallas as pl
from jax.experimental.pallas import tpu as pltpu
from jax.sharding import PartitionSpec as P

DAMP = 0.1
QUERY_VMEM = 56426496
VMEM = 53 * 2**20 + 2**19
QUERY_BITS = (8, 4, 24, 32, 1, 3)
QUERY_AT = {1: 3, 2: 4, 4: 5}
FACTOR_BITS = (1, 3, 4, 24, 8, 32)
HIGH = lax.Precision.HIGHEST


def xor_pairs(size, bit):
    return [(i, i ^ bit) for i in range(size)]


def project_kernel(offset, has_query, x_hbm, g_hbm, pi_hbm, po_hbm, *rest):
    if has_query:
        query_hbm, out, own, xs, gs, pis, pos, sems, block, query_sem = rest
    else:
        out, xs, gs, pis, pos, sems = rest
    rows, wide = out.shape
    rank = wide // 2
    me = lax.axis_index("mp")
    layer = me ^ offset
    copies = [
        pltpu.make_async_copy(source.at[layer], target, sems.at[index])
        for index, (source, target) in enumerate(
            ((pi_hbm, pis), (x_hbm, xs), (po_hbm, pos), (g_hbm, gs))
        )
    ]
    if has_query:
        fetch = pltpu.make_async_copy(query_hbm.at[me, 0], block, query_sem)
        fetch.start()
    for copy in copies:
        copy.start()
    contract = (((1,), (1,)), ((), ()))
    copies[0].wait()
    copies[1].wait()
    out[:, :rank] = lax.dot_general(
        xs[...].reshape(rows, xs.shape[2]), pis[...], contract, preferred_element_type=jnp.float32
    )
    copies[2].wait()
    copies[3].wait()
    out[:, rank:] = lax.dot_general(
        gs[...].reshape(rows, gs.shape[2]), pos[...], contract, preferred_element_type=jnp.float32
    )
    if has_query:
        fetch.wait()
        own[0, :, :rank] = block[: rank // 2]
        own[0, :, rank:] = block[rank // 2 :]


def project(offset, args, query=None, after=None):
    activations, out_grads, proj_in, proj_out = args
    if after is not None:
        proj_in, _ = lax.optimization_barrier((proj_in, after))
    _, clips, frames, width = activations.shape
    hidden = out_grads.shape[3]
    rank = proj_in.shape[1]
    rows = clips * frames
    kind = activations.dtype
    anywhere = pl.BlockSpec(memory_space=pl.ANY)
    vmem = pl.BlockSpec(memory_space=pltpu.VMEM)
    out_shape = jax.ShapeDtypeStruct((rows, 2 * rank), jnp.float32)
    scratch = [
        pltpu.VMEM((clips, frames, width), kind),
        pltpu.VMEM((clips, frames, hidden), kind),
        pltpu.VMEM((rank, width), kind),
        pltpu.VMEM((rank, hidden), kind),
        pltpu.SemaphoreType.DMA((4,)),
    ]
    operands, out_specs = [activations, out_grads, proj_in, proj_out], vmem
    if query is not None:
        operands.append(query)
        out_specs = [vmem, vmem]
        out_shape = [out_shape, jax.ShapeDtypeStruct((1, rank // 2, 2 * rank), jnp.float32)]
        scratch += [pltpu.VMEM((rank, rank), jnp.float32), pltpu.SemaphoreType.DMA]
    return pl.pallas_call(
        functools.partial(project_kernel, offset, query is not None),
        in_specs=[anywhere] * len(operands),
        out_specs=out_specs,
        out_shape=out_shape,
        scratch_shapes=scratch,
        compiler_params=pltpu.CompilerParams(vmem_limit_bytes=VMEM if query is None else QUERY_VMEM),
        cost_estimate=pl.CostEstimate(
            flops=rows * (width + hidden) * rank * 2,
            bytes_accessed=rows * (width + hidden) * 2 + rows * rank * 8,
            transcendentals=0,
        ),
        name="project",
    )(*operands)


def moments_kernel(clips, a_ref, b_ref, fac_ref, grad_ref):
    z = a_ref[...] + b_ref[...]
    rows, wide = z.shape
    rank = wide // 2
    frames = rows // clips
    total = None
    for clip in range(clips):
        part = z[clip * frames : (clip + 1) * frames]
        moment = lax.dot_general(
            part, part, (((0,), (0,)), ((), ())), precision=HIGH, preferred_element_type=jnp.float32
        )
        total = moment if total is None else total + moment
        grad_ref[:, clip * rank : (clip + 1) * rank] = moment[:rank, rank:]
    fac_ref[:, :rank] = total[:rank, :rank]
    fac_ref[:, rank:] = total[rank:, rank:]


def moments(clips, a, b):
    rows, wide = a.shape
    rank = wide // 2
    return pl.pallas_call(
        functools.partial(moments_kernel, clips),
        out_shape=[
            jax.ShapeDtypeStruct((rank, wide), jnp.float32),
            jax.ShapeDtypeStruct((rank, clips * rank), jnp.float32),
        ],
        compiler_params=pltpu.CompilerParams(vmem_limit_bytes=8 * 2**20),
        name="moments",
    )(a, b)


def solve_kernel(clips, total, fa_ref, fb_ref, grad_ref, out_ref):
    rank, wide = fa_ref.shape
    half = rank // 2
    fac = (fa_ref[...] + fb_ref[...]) * (1.0 / total)
    row = lax.broadcasted_iota(jnp.int32, (rank, wide), 0)
    lane = lax.broadcasted_iota(jnp.int32, (rank, wide), 1)
    left = lane < rank
    eye = (row == lane) | (row + rank == lane)
    diag = jnp.where(eye, fac, 0.0)
    trace_l = jnp.sum(jnp.where(left, diag, 0.0))
    trace_r = jnp.sum(jnp.where(left, 0.0, diag))
    shrink = 1.0 / (jnp.where(left, trace_l, trace_r) * (1.0 / rank))
    mat = fac * shrink + jnp.where(eye, DAMP, 0.0)
    def column(source, k):
        return jnp.where(left, source[:, k : k + 1], source[:, rank + k : rank + k + 1])

    c0, c1 = column(mat, 0), column(mat, 1)
    for k in range(0, rank, 2):
        ahead = [column(mat, j) for j in (k + 2, k + 3) if j < rank]
        a, b, d = c0[k : k + 1], c0[k + 1 : k + 2], c1[k + 1 : k + 2]
        at0 = (lane == k) | (lane == rank + k)
        at1 = (lane == k + 1) | (lane == rank + k + 1)
        scale = 1.0 / (a * d - b * b)
        a, b, d = a * scale, b * scale, d * scale
        r0 = jnp.where(at0[:1], 1.0, jnp.where(at1[:1], 0.0, mat[k : k + 1]))
        r1 = jnp.where(at1[:1], 1.0, jnp.where(at0[:1], 0.0, mat[k + 1 : k + 2]))
        n0 = d * r0 - b * r1
        n1 = a * r1 - b * r0
        rest = jnp.where(at0 | at1, 0.0, mat) - c0 * n0 - c1 * n1
        mat = jnp.where(row == k, n0, jnp.where(row == k + 1, n1, rest))
        following = []
        for col in ahead:
            u, v = col[k : k + 1], col[k + 1 : k + 2]
            m0 = d * u - b * v
            m1 = a * v - b * u
            rest = col - c0 * m0 - c1 * m1
            following.append(jnp.where(row == k, m0, jnp.where(row == k + 1, m1, rest)))
        if following:
            c0, c1 = following
    mat = mat * shrink
    inv_in = mat[:, :rank]
    inv_out = mat[:, rank:]
    left_solved = jnp.dot(inv_in, grad_ref[...], precision=HIGH, preferred_element_type=jnp.float32)
    for clip in range(clips):
        solved = jnp.dot(
            left_solved[:, clip * rank : (clip + 1) * rank], inv_out, precision=HIGH,
            preferred_element_type=jnp.float32,
        )
        out_ref[clip, :, :rank] = solved[:half]
        out_ref[clip, :, rank:] = solved[half:]


def solve(clips, total, fa, fb, grads):
    rank, wide = fa.shape
    vmem = pl.BlockSpec(memory_space=pltpu.VMEM)
    return pl.pallas_call(
        functools.partial(solve_kernel, clips, total),
        in_specs=[vmem] * 3,
        out_specs=vmem,
        out_shape=jax.ShapeDtypeStruct((clips, rank // 2, wide), jnp.float32),
        compiler_params=pltpu.CompilerParams(vmem_limit_bytes=8 * 2**20),
        cost_estimate=pl.CostEstimate(flops=0, bytes_accessed=8_000_000, transcendentals=0),
        name="solve",
    )(fa, fb, grads)


def contract_kernel(scale, solved_ref, q_ref, out_ref):
    at = lax.axis_index("dp").astype(jnp.int32)
    queries, half, wide = q_ref.shape
    clips = solved_ref.shape[0]
    q_at = lax.broadcasted_iota(jnp.int32, (queries, queries * 8), 0)
    r_at = lax.broadcasted_iota(jnp.int32, (queries, queries * 8), 1) // 8
    came = at
    for index, bit in enumerate(QUERY_BITS):
        came = came ^ jnp.where((r_at >> index) & 1 == 1, bit, 0)
    select = jnp.where(came == q_at, 1.0, 0.0)
    q = q_ref[...].reshape(queries, half // 8, 8, wide)
    partial = jnp.concatenate(
        [
            jnp.sum(q * solved_ref[clip].reshape(1, half // 8, 8, wide), axis=1).reshape(
                queries * 8, wide
            )
            for clip in range(clips)
        ],
        axis=1,
    )
    per_query = jnp.dot(select, partial, precision=HIGH, preferred_element_type=jnp.float32)
    ones = jnp.full((8, wide), scale, jnp.float32)
    for clip in range(clips):
        line = lax.dot_general(
            ones, per_query[:, clip * wide : (clip + 1) * wide], (((1,), (1,)), ((), ())),
            precision=HIGH, preferred_element_type=jnp.float32,
        )
        out_ref[clip : clip + 1, :] = line[:1]


def contract(scale, solved, queries):
    vmem = pl.BlockSpec(memory_space=pltpu.VMEM)
    return pl.pallas_call(
        functools.partial(contract_kernel, scale),
        in_specs=[vmem] * 2,
        out_specs=vmem,
        out_shape=jax.ShapeDtypeStruct((solved.shape[0], queries.shape[0]), jnp.float32),
        compiler_params=pltpu.CompilerParams(vmem_limit_bytes=16 * 2**20),
        name="contract",
    )(solved, queries)


def local(activations, out_grads, proj_in, proj_out, query_grads):
    layers, clips, frames, _ = activations.shape
    rank = proj_in.shape[1]
    members = lax.axis_size("mp")
    groups = lax.axis_size("dp")
    me = lax.axis_index("mp")

    def widen(blocks, index, after):
        blocks, _ = lax.optimization_barrier((blocks, after))
        pairs = xor_pairs(groups, QUERY_BITS[index])
        return jnp.concatenate([blocks, lax.ppermute(blocks, "dp", pairs)])

    args = (activations, out_grads, proj_in, proj_out)
    far, gathered = project(3, args, query=query_grads)
    far_in = lax.ppermute(far, "mp", xor_pairs(members, 1))
    cross = project(2, args, after=far) + far_in
    cross_in = lax.ppermute(cross, "mp", xor_pairs(members, 2))
    near = project(1, args, after=cross)
    near_in = lax.ppermute(near, "mp", xor_pairs(members, 1))
    mine = project(0, args, after=near)
    gathered = widen(gathered, 0, cross)
    gathered = widen(gathered, 1, near)
    gathered = widen(gathered, 2, mine)
    fac, grads = moments(clips, mine + cross_in, near_in)
    for step, bit in enumerate(FACTOR_BITS[:-1]):
        if step in QUERY_AT:
            gathered = widen(gathered, QUERY_AT[step], fac)
        fac = fac + lax.ppermute(fac, "dp", xor_pairs(groups, bit))
    other = lax.ppermute(fac, "dp", xor_pairs(groups, FACTOR_BITS[-1]))
    solved = solve(clips, clips * frames * groups, fac, other, grads)
    scale = 1.0 / (frames**0.5 * (layers * rank * rank) ** 0.5)
    out = contract(scale, solved, gathered)
    out = out + lax.ppermute(out, "mp", xor_pairs(members, 1))
    return out + lax.ppermute(out, "mp", xor_pairs(members, 2))


def solution(mesh):
    placed = (
        P(None, "dp", None, "mp"),
        P(None, "dp", None, "mp"),
        P(None, None, "mp"),
        P(None, None, "mp"),
        P(None, "dp", None, None),
    )
    return jax.shard_map(
        local, mesh=mesh, in_specs=placed, out_specs=P("dp", None), check_vma=False
    )
```

```python
import functools

import jax
import jax.numpy as jnp
from jax import lax
from jax.experimental import pallas as pl
from jax.experimental.pallas import tpu as pltpu
from jax.sharding import PartitionSpec as P

DAMP = 0.1
VMEM = 53 * 2**20 + 2**19
QUERY_BITS = (8, 4, 24, 32, 1, 3)
QUERY_AT = {1: 3, 2: 4, 4: 5}
FACTOR_BITS = (1, 3, 4, 24, 8, 32)
HIGH = lax.Precision.HIGHEST


def xor_pairs(size, bit):
    return [(i, i ^ bit) for i in range(size)]


def project_kernel(offset, has_query, x_hbm, g_hbm, pi_hbm, po_hbm, *rest):
    if has_query:
        query_hbm, out, own, xs, gs, pis, pos, sems, block, query_sem = rest
    else:
        out, xs, gs, pis, pos, sems = rest
    rows, wide = out.shape
    rank = wide // 2
    me = lax.axis_index("mp")
    layer = me ^ offset
    copies = [
        pltpu.make_async_copy(source.at[layer], target, sems.at[index])
        for index, (source, target) in enumerate(
            ((pi_hbm, pis), (x_hbm, xs), (po_hbm, pos), (g_hbm, gs))
        )
    ]
    if has_query:
        fetch = pltpu.make_async_copy(query_hbm.at[me, 0], block, query_sem)
        fetch.start()
    for copy in copies:
        copy.start()
    contract = (((1,), (1,)), ((), ()))
    copies[0].wait()
    copies[1].wait()
    out[:, :rank] = lax.dot_general(
        xs[...].reshape(rows, xs.shape[2]), pis[...], contract, preferred_element_type=jnp.float32
    )
    copies[2].wait()
    copies[3].wait()
    out[:, rank:] = lax.dot_general(
        gs[...].reshape(rows, gs.shape[2]), pos[...], contract, preferred_element_type=jnp.float32
    )
    if has_query:
        fetch.wait()
        own[0, :, :rank] = block[: rank // 2]
        own[0, :, rank:] = block[rank // 2 :]


def project(offset, args, query=None, after=None):
    activations, out_grads, proj_in, proj_out = args
    if after is not None:
        proj_in, _ = lax.optimization_barrier((proj_in, after))
    _, clips, frames, width = activations.shape
    hidden = out_grads.shape[3]
    rank = proj_in.shape[1]
    rows = clips * frames
    kind = activations.dtype
    anywhere = pl.BlockSpec(memory_space=pl.ANY)
    vmem = pl.BlockSpec(memory_space=pltpu.VMEM)
    out_shape = jax.ShapeDtypeStruct((rows, 2 * rank), jnp.float32)
    scratch = [
        pltpu.VMEM((clips, frames, width), kind),
        pltpu.VMEM((clips, frames, hidden), kind),
        pltpu.VMEM((rank, width), kind),
        pltpu.VMEM((rank, hidden), kind),
        pltpu.SemaphoreType.DMA((4,)),
    ]
    operands, out_specs = [activations, out_grads, proj_in, proj_out], vmem
    if query is not None:
        operands.append(query)
        out_specs = [vmem, vmem]
        out_shape = [out_shape, jax.ShapeDtypeStruct((1, rank // 2, 2 * rank), jnp.float32)]
        scratch += [pltpu.VMEM((rank, rank), jnp.float32), pltpu.SemaphoreType.DMA]
    return pl.pallas_call(
        functools.partial(project_kernel, offset, query is not None),
        in_specs=[anywhere] * len(operands),
        out_specs=out_specs,
        out_shape=out_shape,
        scratch_shapes=scratch,
        compiler_params=pltpu.CompilerParams(vmem_limit_bytes=VMEM),
        cost_estimate=pl.CostEstimate(
            flops=rows * (width + hidden) * rank * 2,
            bytes_accessed=rows * (width + hidden) * 2 + rows * rank * 8,
            transcendentals=0,
        ),
        name="project",
    )(*operands)


def moments_kernel(clips, a_ref, b_ref, fac_ref, grad_ref):
    z = a_ref[...] + b_ref[...]
    rows, wide = z.shape
    rank = wide // 2
    frames = rows // clips
    total = None
    for clip in range(clips):
        part = z[clip * frames : (clip + 1) * frames]
        moment = lax.dot_general(
            part, part, (((0,), (0,)), ((), ())), precision=HIGH, preferred_element_type=jnp.float32
        )
        total = moment if total is None else total + moment
        grad_ref[:, clip * rank : (clip + 1) * rank] = moment[:rank, rank:]
    fac_ref[:, :rank] = total[:rank, :rank]
    fac_ref[:, rank:] = total[rank:, rank:]


def moments(clips, a, b):
    rows, wide = a.shape
    rank = wide // 2
    return pl.pallas_call(
        functools.partial(moments_kernel, clips),
        out_shape=[
            jax.ShapeDtypeStruct((rank, wide), jnp.float32),
            jax.ShapeDtypeStruct((rank, clips * rank), jnp.float32),
        ],
        compiler_params=pltpu.CompilerParams(vmem_limit_bytes=8 * 2**20),
        name="moments",
    )(a, b)


def solve_kernel(clips, total, fa_ref, fb_ref, grad_ref, out_ref):
    rank, wide = fa_ref.shape
    half = rank // 2
    fac = (fa_ref[...] + fb_ref[...]) * (1.0 / total)
    row = lax.broadcasted_iota(jnp.int32, (rank, wide), 0)
    lane = lax.broadcasted_iota(jnp.int32, (rank, wide), 1)
    left = lane < rank
    eye = (row == lane) | (row + rank == lane)
    diag = jnp.where(eye, fac, 0.0)
    trace_l = jnp.sum(jnp.where(left, diag, 0.0))
    trace_r = jnp.sum(jnp.where(left, 0.0, diag))
    shrink = 1.0 / (jnp.where(left, trace_l, trace_r) * (1.0 / rank))
    mat = fac * shrink + jnp.where(eye, DAMP, 0.0)
    def column(source, k):
        return jnp.where(left, source[:, k : k + 1], source[:, rank + k : rank + k + 1])

    c0, c1 = column(mat, 0), column(mat, 1)
    for k in range(0, rank, 2):
        ahead = [column(mat, j) for j in (k + 2, k + 3) if j < rank]
        a, b, d = c0[k : k + 1], c0[k + 1 : k + 2], c1[k + 1 : k + 2]
        at0 = (lane == k) | (lane == rank + k)
        at1 = (lane == k + 1) | (lane == rank + k + 1)
        scale = 1.0 / (a * d - b * b)
        a, b, d = a * scale, b * scale, d * scale
        r0 = jnp.where(at0[:1], 1.0, jnp.where(at1[:1], 0.0, mat[k : k + 1]))
        r1 = jnp.where(at1[:1], 1.0, jnp.where(at0[:1], 0.0, mat[k + 1 : k + 2]))
        n0 = d * r0 - b * r1
        n1 = a * r1 - b * r0
        rest = jnp.where(at0 | at1, 0.0, mat) - c0 * n0 - c1 * n1
        mat = jnp.where(row == k, n0, jnp.where(row == k + 1, n1, rest))
        following = []
        for col in ahead:
            u, v = col[k : k + 1], col[k + 1 : k + 2]
            m0 = d * u - b * v
            m1 = a * v - b * u
            rest = col - c0 * m0 - c1 * m1
            following.append(jnp.where(row == k, m0, jnp.where(row == k + 1, m1, rest)))
        if following:
            c0, c1 = following
    mat = mat * shrink
    inv_in = mat[:, :rank]
    inv_out = mat[:, rank:]
    left_solved = jnp.dot(inv_in, grad_ref[...], precision=HIGH, preferred_element_type=jnp.float32)
    for clip in range(clips):
        solved = jnp.dot(
            left_solved[:, clip * rank : (clip + 1) * rank], inv_out, precision=HIGH,
            preferred_element_type=jnp.float32,
        )
        out_ref[clip, :, :rank] = solved[:half]
        out_ref[clip, :, rank:] = solved[half:]


def solve(clips, total, fa, fb, grads):
    rank, wide = fa.shape
    vmem = pl.BlockSpec(memory_space=pltpu.VMEM)
    return pl.pallas_call(
        functools.partial(solve_kernel, clips, total),
        in_specs=[vmem] * 3,
        out_specs=vmem,
        out_shape=jax.ShapeDtypeStruct((clips, rank // 2, wide), jnp.float32),
        compiler_params=pltpu.CompilerParams(vmem_limit_bytes=8 * 2**20),
        cost_estimate=pl.CostEstimate(flops=0, bytes_accessed=8_000_000, transcendentals=0),
        name="solve",
    )(fa, fb, grads)


def contract_kernel(scale, solved_ref, q_ref, out_ref):
    at = lax.axis_index("dp").astype(jnp.int32)
    queries, half, wide = q_ref.shape
    clips = solved_ref.shape[0]
    q_at = lax.broadcasted_iota(jnp.int32, (queries, queries * 8), 0)
    r_at = lax.broadcasted_iota(jnp.int32, (queries, queries * 8), 1) // 8
    came = at
    for index, bit in enumerate(QUERY_BITS):
        came = came ^ jnp.where((r_at >> index) & 1 == 1, bit, 0)
    select = jnp.where(came == q_at, 1.0, 0.0)
    q = q_ref[...].reshape(queries, half // 8, 8, wide)
    partial = jnp.concatenate(
        [
            jnp.sum(q * solved_ref[clip].reshape(1, half // 8, 8, wide), axis=1).reshape(
                queries * 8, wide
            )
            for clip in range(clips)
        ],
        axis=1,
    )
    per_query = jnp.dot(select, partial, precision=HIGH, preferred_element_type=jnp.float32)
    ones = jnp.full((8, wide), scale, jnp.float32)
    for clip in range(clips):
        line = lax.dot_general(
            ones, per_query[:, clip * wide : (clip + 1) * wide], (((1,), (1,)), ((), ())),
            precision=HIGH, preferred_element_type=jnp.float32,
        )
        out_ref[clip : clip + 1, :] = line[:1]


def contract(scale, solved, queries):
    vmem = pl.BlockSpec(memory_space=pltpu.VMEM)
    return pl.pallas_call(
        functools.partial(contract_kernel, scale),
        in_specs=[vmem] * 2,
        out_specs=vmem,
        out_shape=jax.ShapeDtypeStruct((solved.shape[0], queries.shape[0]), jnp.float32),
        compiler_params=pltpu.CompilerParams(vmem_limit_bytes=16 * 2**20),
        name="contract",
    )(solved, queries)


def local(activations, out_grads, proj_in, proj_out, query_grads):
    layers, clips, frames, _ = activations.shape
    rank = proj_in.shape[1]
    members = lax.axis_size("mp")
    groups = lax.axis_size("dp")
    me = lax.axis_index("mp")

    def widen(blocks, index, after):
        blocks, _ = lax.optimization_barrier((blocks, after))
        pairs = xor_pairs(groups, QUERY_BITS[index])
        return jnp.concatenate([blocks, lax.ppermute(blocks, "dp", pairs)])

    args = (activations, out_grads, proj_in, proj_out)
    far = project(3, args)
    far_in = lax.ppermute(far, "mp", xor_pairs(members, 1))
    cross, gathered = project(2, args, query=query_grads, after=far)
    cross = cross + far_in
    cross_in = lax.ppermute(cross, "mp", xor_pairs(members, 2))
    near = project(1, args, after=cross)
    near_in = lax.ppermute(near, "mp", xor_pairs(members, 1))
    mine = project(0, args, after=near)
    gathered = widen(gathered, 0, cross)
    gathered = widen(gathered, 1, near)
    gathered = widen(gathered, 2, mine)
    fac, grads = moments(clips, mine + cross_in, near_in)
    for step, bit in enumerate(FACTOR_BITS[:-1]):
        if step in QUERY_AT:
            gathered = widen(gathered, QUERY_AT[step], fac)
        fac = fac + lax.ppermute(fac, "dp", xor_pairs(groups, bit))
    other = lax.ppermute(fac, "dp", xor_pairs(groups, FACTOR_BITS[-1]))
    solved = solve(clips, clips * frames * groups, fac, other, grads)
    scale = 1.0 / (frames**0.5 * (layers * rank * rank) ** 0.5)
    out = contract(scale, solved, gathered)
    out = out + lax.ppermute(out, "mp", xor_pairs(members, 1))
    return out + lax.ppermute(out, "mp", xor_pairs(members, 2))


def solution(mesh):
    placed = (
        P(None, "dp", None, "mp"),
        P(None, "dp", None, "mp"),
        P(None, None, "mp"),
        P(None, None, "mp"),
        P(None, "dp", None, None),
    )
    return jax.shard_map(
        local, mesh=mesh, in_specs=placed, out_specs=P("dp", None), check_vma=False
    )
```
